32 devices in a mesh: depth: 2 (over core), row: 4 (over y, x), col: 4 (over z).
Axes of the slice: x: 2, y: 2, z: 4, core: 2. Of those that a mesh axis runs over, the one named last changes fastest.
Arguments:
- activations: bfloat16 [2048, 6144], P('depth', ('row', 'col')), may hold values from -1000 to 1000
- norm_gain: bfloat16 [6144], P(('row', 'col')), may hold values from 0.099609375 to 1.8984375
- up_weight: bfloat16 [6144, 12288], P('row', 'col'), may hold values from -0.078125 to 0.078125
- down_weight: bfloat16 [12288, 6144], P('col', 'row'), may hold values from -0.0546875 to 0.0546875
- upstream: bfloat16 [2048, 6144], P('depth', ('row', 'col')), may hold values from -6 to 6
Outputs:
- branch: bfloat16 [2048, 6144], P('depth', ('row', 'col'))
- grad_input: bfloat16 [2048, 6144], P('depth', ('row', 'col'))
- grad_up: float32 [6144, 12288], P('row', ('col', 'depth'))
- grad_down: float32 [12288, 6144], P('col', ('row', 'depth'))
- grad_gain: float32 [6144], P(('row', 'col', 'depth'))
The draws below stay inside these ranges and needn't reach their ends.
All inputs are finite; a program needn't handle non-finite values.
Results may differ from the reference program's by a relative error of at most 0.018.
Values may be sent and summed in bfloat16 or wider, within the bound.
A program may use at most 192 MiB of HBM per device.

```python
import math
import jax
import jax.numpy as jnp
from jax import lax

D = 6144
FF = 12288
TOKENS = 2048
N_ROW = 4
N_COL = 4


def draw_activations(key, part):
    key = jax.random.fold_in(key, 7)
    noise_key, row_key = jax.random.split(key, 2)
    position = jnp.arange(D, dtype=jnp.float32) / max(D - 1, 1)
    column_scale = jnp.exp(math.log(10.0) * position)
    row_scale = jnp.exp(math.log(10.0) * jax.random.uniform(row_key, (TOKENS, 1), jnp.float32))
    noise = jax.random.normal(noise_key, (TOKENS, D), jnp.float32)
    values = noise * column_scale * row_scale
    return values.astype(jnp.bfloat16)


def level_of(own_key, extent, pieces, low, largest):
    gain = 1.0
    for axis_at, blocks in pieces:
        draws = jax.random.uniform(jax.random.fold_in(jax.random.fold_in(own_key, 6), axis_at), (blocks,), jnp.float32, low / len(pieces), largest / len(pieces))
        gain = gain * jnp.repeat(jnp.exp(draws), extent[axis_at] // blocks).reshape((-1,) + (1,) * (len(extent) - 1 - axis_at))
    return gain


def centred(key, shape, scale, most, cuts=(), kind=jnp.bfloat16):
    values = scale * jax.random.normal(key, shape, jnp.float32)
    if cuts:
        values = values * level_of(key, shape, cuts, -0.22, 0.18)
    return jnp.clip(values, -most, most).astype(kind)


def setup_inputs(seed: int = 0) -> dict:
    key_of = jax.random.split(jax.random.key(seed), 6)
    activations = draw_activations(jax.random.fold_in(key_of[5], 71), 0)
    norm_gain = jnp.clip(1.0 + 0.18 * jax.random.normal(key_of[1], (D,), jnp.float32), 0.099609375, 1.8984375).astype(jnp.bfloat16)
    up_weight = centred(key_of[2], (D, FF), D ** -0.5, 0.078125, ((0, 4), (1, 4)))
    down_weight = centred(key_of[3], (FF, D), FF ** -0.5, 0.0546875, ((0, 4), (1, 4)))
    upstream = centred(key_of[4], (TOKENS, D), 1.0, 6.0, ((0, 2), (1, 16)))
    return {"activations": activations, "norm_gain": norm_gain, "up_weight": up_weight, "down_weight": down_weight, "upstream": upstream}


EPSILON = 1e-06
INV_ROOT2 = 0.7071067811865476
INV_ROOT_TAU = 0.3989422804014327

def gelu_value(values):
    return 0.5 * values * (1.0 + jax.scipy.special.erf(values * INV_ROOT2))

def gelu_slope(values):
    return 0.5 * (1.0 + jax.scipy.special.erf(values * INV_ROOT2)) + values * INV_ROOT_TAU * jnp.exp(-0.5 * values * values)

def block_product(left, right, count):
    width = left.shape[1] // count
    total = jnp.zeros((left.shape[0], right.shape[1]), jnp.float32)
    for block in range(count):
        part = jnp.dot(left[:, block * width:(block + 1) * width], right[block * width:(block + 1) * width, :], preferred_element_type=jnp.float32)
        rounded = lax.optimization_barrier(part.astype(jnp.bfloat16))
        total = total + rounded.astype(jnp.float32)
    return total

def reference(activations, norm_gain, up_weight, down_weight, upstream):
    wide = activations.astype(jnp.float32)
    centre = lax.optimization_barrier(jnp.mean(wide, axis=1, keepdims=True))
    second = lax.optimization_barrier(jnp.mean(wide * wide, axis=1, keepdims=True))
    spread = lax.rsqrt(second - centre * centre + EPSILON)
    whitened = (wide - centre) * spread
    gain_wide = norm_gain.astype(jnp.float32)
    normed = (whitened * gain_wide).astype(jnp.bfloat16)
    pre_act = block_product(normed, up_weight, N_ROW)
    activated = gelu_value(pre_act).astype(jnp.bfloat16)
    branch = block_product(activated, down_weight, N_COL).astype(jnp.bfloat16)
    grad_pre = block_product(upstream, jnp.transpose(down_weight), N_ROW)
    gated = (grad_pre * gelu_slope(pre_act)).astype(jnp.bfloat16)
    grad_down = jnp.dot(jnp.transpose(activated), upstream, preferred_element_type=jnp.float32)
    grad_up = jnp.dot(jnp.transpose(normed), gated, preferred_element_type=jnp.float32)
    grad_normed = block_product(gated, jnp.transpose(up_weight), N_COL)
    scaled = grad_normed * gain_wide
    mean_grad = lax.optimization_barrier(jnp.mean(scaled, axis=1, keepdims=True))
    mean_cross = lax.optimization_barrier(jnp.mean(scaled * whitened, axis=1, keepdims=True))
    grad_input = (spread * (scaled - mean_grad - whitened * mean_cross)).astype(jnp.bfloat16)
    grad_gain = lax.optimization_barrier(jnp.sum(grad_normed * whitened, axis=0))
    return (branch, grad_input, grad_up, grad_down, grad_gain)
```

```python
import jax
import jax.numpy as jnp
from jax import lax
from jax.sharding import PartitionSpec as P

D = 6144
CHUNKS = 2
LAG = 2


EPSILON = 1e-06
INV_ROOT2 = 0.7071067811865476
INV_ROOT_TAU = 0.3989422804014327


def gelu_value(values):
    return 0.5 * values * (1.0 + jax.scipy.special.erf(values * INV_ROOT2))


def gelu_slope(values):
    return 0.5 * (
        1.0 + jax.scipy.special.erf(values * INV_ROOT2)
    ) + values * INV_ROOT_TAU * jnp.exp(-0.5 * values * values)


def inner_rows(left, right):
    return lax.dot_general(
        left, right, (((0,), (0,)), ((), ())), preferred_element_type=jnp.float32
    )


def inner_cols(left, right):
    return lax.dot_general(
        left, right, (((1,), (1,)), ((), ())), preferred_element_type=jnp.float32
    )


def plain_body(activations, norm_gain, up_weight, down_weight, upstream):
    shard_width = activations.shape[1]
    gain_local = norm_gain.astype(jnp.float32)
    local = activations.astype(jnp.float32)
    first, second = lax.psum(
        (jnp.sum(local, axis=1), jnp.sum(local * local, axis=1)), ("row", "col")
    )
    centre = (first / D)[:, None]
    spread = lax.rsqrt(second[:, None] / D - centre * centre + EPSILON)
    whitened = (local - centre) * spread
    normed = lax.all_gather((whitened * gain_local).astype(jnp.bfloat16), "col", axis=1, tiled=True)
    partial_up = jnp.dot(normed, up_weight, preferred_element_type=jnp.float32)
    pre_act = lax.psum_scatter(
        partial_up.astype(jnp.bfloat16), "row", scatter_dimension=1, tiled=True
    ).astype(jnp.float32)
    activated = lax.all_gather(gelu_value(pre_act).astype(jnp.bfloat16), "row", axis=1, tiled=True)
    partial_down = jnp.dot(activated, down_weight, preferred_element_type=jnp.float32)
    branch = lax.psum_scatter(
        partial_down.astype(jnp.bfloat16), "col", scatter_dimension=1, tiled=True
    )
    grad_rows = lax.all_gather(upstream, "col", axis=1, tiled=True)
    grad_down_local = inner_rows(activated, grad_rows)
    partial_hidden = inner_cols(grad_rows, down_weight)
    grad_pre = lax.psum_scatter(
        partial_hidden.astype(jnp.bfloat16), "row", scatter_dimension=1, tiled=True
    ).astype(jnp.float32)
    gated = lax.all_gather(
        (grad_pre * gelu_slope(pre_act)).astype(jnp.bfloat16), "row", axis=1, tiled=True
    )
    grad_up_local = inner_rows(normed, gated)
    partial_normed = inner_cols(gated, up_weight)
    grad_normed = lax.psum_scatter(
        partial_normed.astype(jnp.bfloat16), "col", scatter_dimension=1, tiled=True
    ).astype(jnp.float32)
    scaled = grad_normed * gain_local
    total_grad, total_cross = lax.psum(
        (jnp.sum(scaled, axis=1), jnp.sum(scaled * whitened, axis=1)), ("row", "col")
    )
    mean_grad = (total_grad / D)[:, None]
    mean_cross = (total_cross / D)[:, None]
    grad_input = (spread * (scaled - mean_grad - whitened * mean_cross)).astype(jnp.bfloat16)
    gain_part = jnp.sum(grad_normed * whitened, axis=0).reshape(1, shard_width)
    grad_up, grad_down, gain_total = (
        lax.psum_scatter(
            grad_up_local.astype(jnp.bfloat16), "depth", scatter_dimension=1, tiled=True
        ).astype(jnp.float32),
        lax.psum_scatter(
            grad_down_local.astype(jnp.bfloat16), "depth", scatter_dimension=1, tiled=True
        ).astype(jnp.float32),
        lax.psum_scatter(
            gain_part.astype(jnp.bfloat16), "depth", scatter_dimension=1, tiled=True
        ).astype(jnp.float32),
    )
    return (branch, grad_input, grad_up, grad_down, gain_total.reshape(-1))


def take_block(values, axis, index, width):
    return lax.dynamic_slice_in_dim(values, index * width, width, axis)


def reorder(values, axis, order, width):
    return jnp.concatenate([take_block(values, axis, index, width) for index in order], axis=axis)


RING_UP = [(0, 1), (1, 2), (2, 3), (3, 0)]
RING_DOWN = [(0, 3), (1, 0), (2, 1), (3, 2)]
RING_TWO = [(0, 2), (1, 3), (2, 0), (3, 1)]


def over_x(values):
    return lax.ppermute(values, "row", [(0, 1), (1, 0), (2, 3), (3, 2)])


def over_y(values):
    return lax.ppermute(values, "row", [(0, 2), (2, 0), (1, 3), (3, 1)])


def over_core(values):
    return lax.ppermute(values, "depth", [(0, 1), (1, 0)])


def total_over_slice(values):
    values = values + over_x(values)
    values = values + over_y(values)
    return (
        values
        + lax.ppermute(values, "col", RING_UP)
        + lax.ppermute(values, "col", RING_DOWN)
        + lax.ppermute(values, "col", RING_TWO)
    )


def gather_col(values):
    pieces = [values]
    for _ in range(3):
        pieces.append(lax.ppermute(pieces[-1], "col", RING_DOWN))
    return pieces


def scatter_col(partial):
    width = partial.shape[1] // 4
    block = lambda j: partial[:, j * width:(j + 1) * width]
    moving = block(3)
    for j in (2, 1, 0):
        moving = block(j).astype(jnp.float32) + lax.ppermute(moving, "col", RING_UP).astype(jnp.float32)
        if j:
            moving = moving.astype(jnp.bfloat16)
    return moving


def gather_row(values):
    half = values.shape[0] // 2
    top, low = values[:half], values[half:]
    top_x, low_y = over_x(top), over_y(low)
    top_y, low_x = over_y(top), over_x(low)
    return jnp.concatenate(
        [
            jnp.concatenate([top, top_x, top_y, over_y(top_x)], axis=1),
            jnp.concatenate([low, low_x, low_y, over_x(low_y)], axis=1),
        ],
        axis=0,
    )


def scatter_row(partial):
    half, width = partial.shape[0] // 2, partial.shape[1] // 4
    top = lambda j: partial[:half, j * width:(j + 1) * width]
    low = lambda j: partial[half:, j * width:(j + 1) * width]
    wide = lambda values: values.astype(jnp.float32)
    top_far, low_far = over_x(top(3)), over_y(low(3))
    top_near, low_near = over_x(top(1)), over_y(low(2))
    top_last = over_y((wide(top(2)) + wide(top_far)).astype(jnp.bfloat16))
    low_last = over_x((wide(low(1)) + wide(low_far)).astype(jnp.bfloat16))
    return jnp.concatenate(
        [
            wide(top(0)) + wide(top_near) + wide(top_last),
            wide(low(0)) + wide(low_near) + wide(low_last),
        ],
        axis=0,
    )


def after(values, earlier):
    return lax.optimization_barrier((values, earlier))[0]


def body(activations, norm_gain, up_weight, down_weight, upstream):
    tokens, shard = activations.shape
    row, col, core = lax.axis_index("row"), lax.axis_index("col"), lax.axis_index("depth")
    hidden = up_weight.shape[1] // 4
    turned = [lax.rem(col + j, 4) for j in range(4)]
    turned_back = [lax.rem(j - col + 4, 4) for j in range(4)]
    flipped = [row ^ j for j in range(4)]

    local = activations.astype(jnp.float32)
    sums = total_over_slice(
        jnp.stack([jnp.sum(local, axis=1), jnp.sum(local * local, axis=1)], axis=0)
    )
    gain_local = norm_gain.astype(jnp.float32).reshape(1, shard)
    gain_block = jnp.concatenate(gather_col(gain_local), axis=1)
    centre = (sums[0] / D)[:, None]
    spread = lax.rsqrt(sums[1][:, None] / D - centre * centre + EPSILON)

    up = reorder(reorder(up_weight, 0, turned, shard), 1, flipped, hidden)
    down = reorder(reorder(down_weight, 1, turned, shard), 0, flipped, hidden)

    size = tokens // CHUNKS
    parts = [slice(k * size, (k + 1) * size) for k in range(CHUNKS)]
    behind = None
    grad_rows, raw = [], []
    for part in parts:
        for source, store in ((upstream, grad_rows), (activations, raw)):
            piece = source[part]
            if behind is not None:
                piece = after(piece, behind)
            pieces = gather_col(piece)
            behind = pieces[LAG]
            store.append(jnp.concatenate(pieces, axis=1))

    whitened, normed, activated, gated, branch, grad_normed, sums_back = ([] for _ in range(7))
    for k, part in enumerate(parts):
        grad_pre = scatter_row(inner_cols(grad_rows[k], down).astype(jnp.bfloat16))
        whitened.append((raw[k].astype(jnp.float32) - centre[part]) * spread[part])
        normed.append((whitened[k] * gain_block).astype(jnp.bfloat16))
        pre_act = scatter_row(
            jnp.dot(normed[k], up, preferred_element_type=jnp.float32).astype(jnp.bfloat16)
        )
        activated.append(gather_row(gelu_value(pre_act).astype(jnp.bfloat16)))
        gated.append(gather_row((grad_pre * gelu_slope(pre_act)).astype(jnp.bfloat16)))
        branch.append(
            scatter_col(
                jnp.dot(activated[k], down, preferred_element_type=jnp.float32).astype(jnp.bfloat16)
            ).astype(jnp.bfloat16)
        )
        partial = inner_cols(gated[k], up).astype(jnp.bfloat16)
        wide = partial.astype(jnp.float32) * gain_block
        sums_back.append(
            total_over_slice(
                jnp.stack([jnp.sum(wide, axis=1), jnp.sum(wide * whitened[k], axis=1)], axis=0)
            )
        )
        grad_normed.append(scatter_col(partial))

    def over_tokens(blocks, axis_order, width):
        return jnp.concatenate([reorder(block, 1, axis_order, width) for block in blocks], axis=0)

    def split(order):
        keep = [jnp.where(core == 0, order[b], order[2 + b]) for b in range(2)]
        send = [jnp.where(core == 0, order[2 + b], order[b]) for b in range(2)]
        return keep, send

    hidden_keep, hidden_send = split(flipped)
    width_keep, width_send = split(turned_back)

    whole_activated = over_tokens(activated, flipped, hidden)
    down_send = inner_rows(whole_activated, over_tokens(grad_rows, width_send, shard))
    down_got = over_core(down_send.astype(jnp.bfloat16))
    grad_down = inner_rows(
        whole_activated, over_tokens(grad_rows, width_keep, shard)
    ) + down_got.astype(jnp.float32)

    whole_normed = over_tokens(normed, turned_back, shard)
    up_send = inner_rows(whole_normed, over_tokens(gated, hidden_send, hidden))
    up_got = over_core(up_send.astype(jnp.bfloat16))
    grad_up = inner_rows(
        whole_normed, over_tokens(gated, hidden_keep, hidden)
    ) + up_got.astype(jnp.float32)

    grad_input, gain_part = [], 0.0
    for k, part in enumerate(parts):
        white = (local[part] - centre[part]) * spread[part]
        scaled = grad_normed[k] * gain_local
        mean_grad = (sums_back[k][0] / D)[:, None]
        mean_cross = (sums_back[k][1] / D)[:, None]
        grad_input.append(
            (spread[part] * (scaled - mean_grad - white * mean_cross)).astype(jnp.bfloat16)
        )
        gain_part = gain_part + jnp.sum(grad_normed[k] * white, axis=0, keepdims=True)
    half = shard // 2
    gain_total = take_block(gain_part, 1, core, half) + over_core(
        take_block(gain_part, 1, 1 - core, half)
    )
    return (
        jnp.concatenate(branch, axis=0),
        jnp.concatenate(grad_input, axis=0),
        grad_up,
        grad_down,
        gain_total.reshape(-1),
    )


def solution(mesh):
    in_specs = (
        P("depth", ("row", "col")),
        P(("row", "col")),
        P("row", "col"),
        P("col", "row"),
        P("depth", ("row", "col")),
    )
    out_specs = (
        P("depth", ("row", "col")),
        P("depth", ("row", "col")),
        P("row", ("col", "depth")),
        P("col", ("row", "depth")),
        P(("row", "col", "depth")),
    )
    paired = mesh.shape["row"] == 4 and mesh.shape["col"] == 4 and mesh.shape["depth"] == 2
    return jax.shard_map(body if paired else plain_body, mesh=mesh, in_specs=in_specs, out_specs=out_specs, check_vma=False)
```

```python
import jax
import jax.numpy as jnp
from jax import lax
from jax.sharding import PartitionSpec as P

D = 6144
CHUNKS = 2


EPSILON = 1e-06
INV_ROOT2 = 0.7071067811865476
INV_ROOT_TAU = 0.3989422804014327


def gelu_value(values):
    return 0.5 * values * (1.0 + jax.scipy.special.erf(values * INV_ROOT2))


def gelu_slope(values):
    return 0.5 * (
        1.0 + jax.scipy.special.erf(values * INV_ROOT2)
    ) + values * INV_ROOT_TAU * jnp.exp(-0.5 * values * values)


def inner_rows(left, right):
    return lax.dot_general(
        left, right, (((0,), (0,)), ((), ())), preferred_element_type=jnp.float32
    )


def inner_cols(left, right):
    return lax.dot_general(
        left, right, (((1,), (1,)), ((), ())), preferred_element_type=jnp.float32
    )


def plain_body(activations, norm_gain, up_weight, down_weight, upstream):
    shard_width = activations.shape[1]
    gain_local = norm_gain.astype(jnp.float32)
    local = activations.astype(jnp.float32)
    first, second = lax.psum(
        (jnp.sum(local, axis=1), jnp.sum(local * local, axis=1)), ("row", "col")
    )
    centre = (first / D)[:, None]
    spread = lax.rsqrt(second[:, None] / D - centre * centre + EPSILON)
    whitened = (local - centre) * spread
    normed = lax.all_gather((whitened * gain_local).astype(jnp.bfloat16), "col", axis=1, tiled=True)
    partial_up = jnp.dot(normed, up_weight, preferred_element_type=jnp.float32)
    pre_act = lax.psum_scatter(
        partial_up.astype(jnp.bfloat16), "row", scatter_dimension=1, tiled=True
    ).astype(jnp.float32)
    activated = lax.all_gather(gelu_value(pre_act).astype(jnp.bfloat16), "row", axis=1, tiled=True)
    partial_down = jnp.dot(activated, down_weight, preferred_element_type=jnp.float32)
    branch = lax.psum_scatter(
        partial_down.astype(jnp.bfloat16), "col", scatter_dimension=1, tiled=True
    )
    grad_rows = lax.all_gather(upstream, "col", axis=1, tiled=True)
    grad_down_local = inner_rows(activated, grad_rows)
    partial_hidden = inner_cols(grad_rows, down_weight)
    grad_pre = lax.psum_scatter(
        partial_hidden.astype(jnp.bfloat16), "row", scatter_dimension=1, tiled=True
    ).astype(jnp.float32)
    gated = lax.all_gather(
        (grad_pre * gelu_slope(pre_act)).astype(jnp.bfloat16), "row", axis=1, tiled=True
    )
    grad_up_local = inner_rows(normed, gated)
    partial_normed = inner_cols(gated, up_weight)
    grad_normed = lax.psum_scatter(
        partial_normed.astype(jnp.bfloat16), "col", scatter_dimension=1, tiled=True
    ).astype(jnp.float32)
    scaled = grad_normed * gain_local
    total_grad, total_cross = lax.psum(
        (jnp.sum(scaled, axis=1), jnp.sum(scaled * whitened, axis=1)), ("row", "col")
    )
    mean_grad = (total_grad / D)[:, None]
    mean_cross = (total_cross / D)[:, None]
    grad_input = (spread * (scaled - mean_grad - whitened * mean_cross)).astype(jnp.bfloat16)
    gain_part = jnp.sum(grad_normed * whitened, axis=0).reshape(1, shard_width)
    grad_up, grad_down, gain_total = (
        lax.psum_scatter(
            grad_up_local.astype(jnp.bfloat16), "depth", scatter_dimension=1, tiled=True
        ).astype(jnp.float32),
        lax.psum_scatter(
            grad_down_local.astype(jnp.bfloat16), "depth", scatter_dimension=1, tiled=True
        ).astype(jnp.float32),
        lax.psum_scatter(
            gain_part.astype(jnp.bfloat16), "depth", scatter_dimension=1, tiled=True
        ).astype(jnp.float32),
    )
    return (branch, grad_input, grad_up, grad_down, gain_total.reshape(-1))


def take_block(values, axis, index, width):
    return lax.dynamic_slice_in_dim(values, index * width, width, axis)


def place(rows, width, pieces):
    whole = jnp.zeros((rows, 4 * width), pieces[0][0].dtype)
    for values, at, index in pieces:
        whole = lax.dynamic_update_slice(whole, values, (at, index * width))
    return whole


RING_UP = [(0, 1), (1, 2), (2, 3), (3, 0)]
RING_DOWN = [(0, 3), (1, 0), (2, 1), (3, 2)]
RING_TWO = [(0, 2), (1, 3), (2, 0), (3, 1)]


def over_x(values):
    return lax.ppermute(values, "row", [(0, 1), (1, 0), (2, 3), (3, 2)])


def over_y(values):
    return lax.ppermute(values, "row", [(0, 2), (2, 0), (1, 3), (3, 1)])


def over_core(values):
    return lax.ppermute(values, "depth", [(0, 1), (1, 0)])


def total_over_slice(values):
    values = values + over_x(values)
    values = values + over_y(values)
    return (
        values
        + lax.ppermute(values, "col", RING_UP)
        + lax.ppermute(values, "col", RING_DOWN)
        + lax.ppermute(values, "col", RING_TWO)
    )


def gather_col(values, owners):
    pieces = [values]
    for _ in range(3):
        pieces.append(lax.ppermute(pieces[-1], "col", RING_DOWN))
    rows, width = values.shape
    return place(rows, width, [(p, 0, o) for p, o in zip(pieces, owners)]), pieces


def scatter_col(partial, owners):
    width = partial.shape[1] // 4
    block = lambda j: take_block(partial, 1, owners[j], width)
    moving, arrived = block(3), []
    for j in (2, 1, 0):
        arrived.append(lax.ppermute(moving, "col", RING_UP))
        moving = block(j).astype(jnp.float32) + arrived[-1].astype(jnp.float32)
        if j:
            moving = moving.astype(jnp.bfloat16)
    return moving, arrived


def gather_row(values, owners):
    rows, width = values.shape
    half = rows // 2
    top, low = values[:half], values[half:]
    top_x, low_y = over_x(top), over_y(low)
    top_y, low_x = over_y(top), over_x(low)
    upper = [top, top_x, top_y, over_y(top_x)]
    lower = [low, low_x, low_y, over_x(low_y)]
    return place(
        rows,
        width,
        [(p, 0, o) for p, o in zip(upper, owners)] + [(p, half, o) for p, o in zip(lower, owners)],
    ), upper


def scatter_row(partial, owners):
    half, width = partial.shape[0] // 2, partial.shape[1] // 4
    top = lambda j: take_block(partial[:half], 1, owners[j], width)
    low = lambda j: take_block(partial[half:], 1, owners[j], width)
    wide = lambda values: values.astype(jnp.float32)
    top_far, low_far = over_x(top(3)), over_y(low(3))
    top_near, low_near = over_x(top(1)), over_y(low(2))
    top_last = over_y((wide(top(2)) + wide(top_far)).astype(jnp.bfloat16))
    low_last = over_x((wide(low(1)) + wide(low_far)).astype(jnp.bfloat16))
    return jnp.concatenate(
        [
            wide(top(0)) + wide(top_near) + wide(top_last),
            wide(low(0)) + wide(low_near) + wide(low_last),
        ],
        axis=0,
    )


fixed = lax.optimization_barrier


def after(values, earlier):
    return lax.optimization_barrier((values, earlier))[0]


def body(activations, norm_gain, up_weight, down_weight, upstream):
    tokens, shard = activations.shape
    row, col, core = lax.axis_index("row"), lax.axis_index("col"), lax.axis_index("depth")
    hidden = up_weight.shape[1] // 4
    turned = [lax.rem(col + j, 4) for j in range(4)]
    flipped = [row ^ j for j in range(4)]

    local = activations.astype(jnp.float32)
    sums = total_over_slice(
        jnp.stack([jnp.sum(local, axis=1), jnp.sum(local * local, axis=1)], axis=0)
    )
    gain_local = norm_gain.astype(jnp.float32).reshape(1, shard)
    gain_block = gather_col(gain_local, turned)[0]
    centre = (sums[0] / D)[:, None]
    spread = lax.rsqrt(sums[1][:, None] / D - centre * centre + EPSILON)

    up, down = up_weight, down_weight

    size = tokens // CHUNKS
    parts = [slice(k * size, (k + 1) * size) for k in range(CHUNKS)]
    behind = None
    grad_rows, raw = [], []
    for part in parts:
        for source, store, lag in ((upstream, grad_rows, 1), (activations, raw, 3)):
            piece = source[part]
            if behind is not None:
                piece = after(piece, behind)
            whole, pieces = gather_col(piece, turned)
            behind = pieces[lag]
            store.append(fixed(whole))

    whitened, normed, activated, gated, branch, grad_normed, sums_back = ([] for _ in range(7))
    marks = []
    down_sent, down_kept = [], []

    def half_product(left, right, half_at):
        return inner_rows(left, take_block(right, 1, half_at, right.shape[1] // 2))

    for k, part in enumerate(parts):
        partial_hidden = inner_cols(grad_rows[k], down).astype(jnp.bfloat16)
        if marks:
            partial_hidden = after(partial_hidden, marks[0])
        grad_pre = scatter_row(partial_hidden, flipped)
        whitened.append((raw[k].astype(jnp.float32) - centre[part]) * spread[part])
        normed.append(fixed((whitened[k] * gain_block).astype(jnp.bfloat16)))
        partial_up = jnp.dot(normed[k], up, preferred_element_type=jnp.float32).astype(jnp.bfloat16)
        if marks:
            partial_up = after(partial_up, marks[1])
        pre_act = scatter_row(partial_up, flipped)
        own_activated = fixed(gelu_value(pre_act).astype(jnp.bfloat16))
        if marks:
            own_activated = after(own_activated, marks[2])
        whole, _ = gather_row(own_activated, flipped)
        activated.append(fixed(whole))
        own_gated = fixed((grad_pre * gelu_slope(pre_act)).astype(jnp.bfloat16))
        if marks:
            own_gated = after(own_gated, marks[3])
        whole, hops = gather_row(own_gated, flipped)
        gated.append(fixed(whole))
        summed, branch_steps = scatter_col(
            jnp.dot(activated[k], down, preferred_element_type=jnp.float32).astype(jnp.bfloat16),
            turned,
        )
        branch.append(summed.astype(jnp.bfloat16))
        down_sent.append(half_product(activated[k], grad_rows[k], 1 - core))
        down_kept.append(half_product(activated[k], grad_rows[k], core))
        partial = inner_cols(gated[k], up).astype(jnp.bfloat16)
        wide = partial.astype(jnp.float32) * gain_block
        sums_back.append(
            jnp.stack([jnp.sum(wide, axis=1), jnp.sum(wide * whitened[k], axis=1)], axis=0)
        )
        summed, back_steps = scatter_col(partial, turned)
        grad_normed.append(summed)
        marks = [hops[1], branch_steps[0], (branch_steps[2], back_steps[0]), back_steps[1]]

    totals_back = total_over_slice(jnp.concatenate(sums_back, axis=1))

    down_got = over_core(sum(down_sent).astype(jnp.bfloat16))
    grad_down = sum(down_kept) + down_got.astype(jnp.float32)
    late = [after(b, back_steps[0]) for b in gated]
    later = [after(b, back_steps[1]) for b in gated]
    up_sent = sum(half_product(a, b, 1 - core) for a, b in zip(normed, late))
    up_got = over_core(up_sent.astype(jnp.bfloat16))
    grad_up = sum(half_product(a, b, core) for a, b in zip(normed, later)) + up_got.astype(
        jnp.float32
    )

    grad_input, gain_part = [], 0.0
    for k, part in enumerate(parts):
        white = (local[part] - centre[part]) * spread[part]
        scaled = grad_normed[k] * gain_local
        mean_grad = (totals_back[0][part] / D)[:, None]
        mean_cross = (totals_back[1][part] / D)[:, None]
        grad_input.append(
            (spread[part] * (scaled - mean_grad - white * mean_cross)).astype(jnp.bfloat16)
        )
        gain_part = gain_part + jnp.sum(grad_normed[k] * white, axis=0, keepdims=True)
    half = shard // 2
    gain_total = take_block(gain_part, 1, core, half) + over_core(
        take_block(gain_part, 1, 1 - core, half)
    )
    return (
        jnp.concatenate(branch, axis=0),
        jnp.concatenate(grad_input, axis=0),
        grad_up,
        grad_down,
        gain_total.reshape(-1),
    )


def solution(mesh):
    in_specs = (
        P("depth", ("row", "col")),
        P(("row", "col")),
        P("row", "col"),
        P("col", "row"),
        P("depth", ("row", "col")),
    )
    out_specs = (
        P("depth", ("row", "col")),
        P("depth", ("row", "col")),
        P("row", ("col", "depth")),
        P("col", ("row", "depth")),
        P(("row", "col", "depth")),
    )
    paired = mesh.shape["row"] == 4 and mesh.shape["col"] == 4 and mesh.shape["depth"] == 2
    return jax.shard_map(body if paired else plain_body, mesh=mesh, in_specs=in_specs, out_specs=out_specs, check_vma=False)
```
